768 devices in a mesh: srv: 384 (over z, y, x), head: 2 (over core).
Axes of the slice: x: 4, y: 8, z: 12, core: 2. Of those that a mesh axis runs over, the one named last changes fastest.
Arguments:
- tokens: bfloat16 [98304, 4096], P(('srv', 'head')), may hold values from -10.5 to 10.5
- doc_ids: int32 [98304], P(('srv', 'head')), may hold values from 0 to 383, never falling along the last dimension, each value on 1 to 512 neighbouring positions
- w_query: bfloat16 [4096, 2048], P(None, 'head'), may hold values from -1 to 1
- w_key: bfloat16 [4096, 512], P(None, 'head'), may hold values from -1.5 to 1.5
- value_weight: bfloat16 [4096, 512], P(None, 'head'), may hold values from -0.09375 to 0.09375
Outputs:
- attended: bfloat16 [98304, 2048], P(('srv', 'head'))
The draws below stay inside these ranges and needn't reach their ends.
Inputs may be any that keep to these rules, and one draw needn't show every extreme that they name: `doc_ids`: documents are consecutive runs of at most 512 tokens; one has exactly that many.
All inputs are finite; a program needn't handle non-finite values.
Results may differ from the reference program's by a relative error of at most 0.012.
The reference program's roundings to bfloat16 on the way count: a program that leaves them out, or rounds other values in their place, can miss the bound.
Values may be sent and summed in bfloat16 or wider, within the bound.
No kernel may reach another device: no remote copies, remote signals or barrier semaphores. Data moves between devices by JAX's collectives and lax.ppermute only.
A program may use at most 64 MiB of HBM per device.

```python
import math
import jax
import jax.numpy as jnp
import numpy as np
from jax import lax

MODEL_WIDTH = 4096
QUERY_HEADS = 16
KEY_VALUE_HEADS = 4
HEAD_SIZE = 128
SPAN = 2
TOK_DEV = 128
GROUP_TOK = 256
TOKENS = 98304
DOCS = 384
N_HEAD = 2


def shared_query(key):
    return jax.random.truncated_normal(key, -6.0, 6.0, (MODEL_WIDTH, QUERY_HEADS * HEAD_SIZE), jnp.float32) * MODEL_WIDTH ** (-0.5)


def draw_w_query(key, part):
    return shared_query(key).astype(jnp.bfloat16)


def draw_w_key(key, part):
    key = jax.random.fold_in(key, 7)
    local_portion = jax.random.truncated_normal(key, -6.0, 6.0, (MODEL_WIDTH, KEY_VALUE_HEADS * HEAD_SIZE), jnp.float32) * MODEL_WIDTH ** (-0.5)
    return local_portion.astype(jnp.bfloat16)


def draw_tokens(key, part):
    key = jax.random.fold_in(key, 3)
    entry_key = jax.random.fold_in(key, 0)
    return jax.random.truncated_normal(entry_key, -6.0, 6.0, (TOKENS, MODEL_WIDTH), jnp.float32).astype(jnp.bfloat16)


def level_of(stream_key, dims, cuts, smallest, high):
    def one(dim, shards_of):
        heights = jax.random.uniform(jax.random.fold_in(jax.random.fold_in(stream_key, 6), dim), (shards_of,), jnp.float32, smallest / len(cuts), high / len(cuts))
        return jnp.repeat(jnp.exp(heights), dims[dim] // shards_of).reshape((-1,) + (1,) * (len(dims) - dim - 1))

    gain = one(*cuts[0])
    for cut in cuts[1:]:
        gain = gain * one(*cut)
    return gain


def profile(amount, total, reach, slope):
    loads = [(1 << 20) // math.isqrt(rank ** slope) + 1 for rank in range(2, amount + 1)]
    rest, holding = total - reach - (amount - 1), [1] * (amount - 1)
    while rest > 0:
        movable = [i for i in range(amount - 1) if holding[i] < reach]
        whole, remaining = sum([loads[i] for i in movable]), rest
        for i in movable:
            extra = min(reach - holding[i], max(1, remaining * loads[i] // whole), rest)
            holding[i] = holding[i] + extra
            rest = rest - extra
    return np.array([reach] + holding)


def ragged_sizes(key, number_of, total, reach, lean):
    if number_of == 2:
        one = jax.random.randint(key, (), max(1, total - reach), min(reach, total - 1) + 1)
        return jnp.stack([one, total - one])
    lengths = jnp.asarray(profile(number_of, total, reach, lean), jnp.int32)
    pairs = (number_of - 1) // 2
    source_of, taker = lengths[1:1 + 2 * pairs:2], lengths[2:2 + 2 * pairs:2]
    room = jnp.minimum(source_of - 1, reach - taker)
    shifted = jax.random.randint(jax.random.fold_in(key, 1), (pairs,), 0, 1 << 20) % (room + 1)
    lengths = lengths.at[1:1 + 2 * pairs:2].set(source_of - shifted).at[2:2 + 2 * pairs:2].set(taker + shifted)
    return lengths[jax.random.permutation(jax.random.fold_in(key, 2), number_of)]


def gaussian(own_key, shape, width, bound, pieces=(), kind=jnp.bfloat16):
    values = width * jax.random.normal(own_key, shape, jnp.float32)
    if pieces:
        values = values * level_of(own_key, shape, pieces, -0.22, 0.18)
    return jnp.clip(values, -bound, bound).astype(kind)


def setup_inputs(seed: int = 0) -> dict:
    seeds = jax.random.split(jax.random.key(seed), 6)
    tokens = draw_tokens(jax.random.fold_in(seeds[5], 71), 0)
    doc_ids = jnp.searchsorted(jnp.cumsum(ragged_sizes(seeds[1], DOCS, TOKENS, SPAN * GROUP_TOK, 2)), jnp.arange(TOKENS), side="right").astype(jnp.int32)
    w_query = draw_w_query(jax.random.fold_in(seeds[5], 71), 0)
    w_key = draw_w_key(jax.random.fold_in(seeds[5], 71), 0)
    value_weight = gaussian(seeds[4], (MODEL_WIDTH, KEY_VALUE_HEADS * HEAD_SIZE), MODEL_WIDTH ** -0.5, 0.09375, ((1, 2),))
    return dict(tokens=tokens, doc_ids=doc_ids, w_query=w_query, w_key=w_key, value_weight=value_weight)


def reference(tokens, doc_ids, w_query, w_key, value_weight):
    group_token = TOK_DEV * N_HEAD
    groups = TOKENS // group_token
    repeat_factor = QUERY_HEADS // KEY_VALUE_HEADS
    query_row_set = jnp.dot(tokens, w_query, preferred_element_type=jnp.float32).astype(jnp.bfloat16)
    key_matrix_rows = jnp.dot(tokens, w_key, preferred_element_type=jnp.float32).astype(jnp.bfloat16)
    value_matrix_rows = jnp.dot(tokens, value_weight, preferred_element_type=jnp.float32).astype(jnp.bfloat16)
    leading_padding = SPAN * group_token
    key_padding = jnp.concatenate([jnp.zeros((leading_padding, KEY_VALUE_HEADS * HEAD_SIZE), jnp.bfloat16), key_matrix_rows], 0)
    value_padding = jnp.concatenate([jnp.zeros((leading_padding, KEY_VALUE_HEADS * HEAD_SIZE), jnp.bfloat16), value_matrix_rows], 0)
    doc_index = doc_ids.astype(jnp.int32)
    doc_pad = jnp.concatenate([jnp.full((leading_padding,), -1, jnp.int32), doc_index], 0)
    key_span_width = (SPAN + 1) * group_token
    logit_scale = 1.0 / (HEAD_SIZE ** 0.5)

    def one_group(group_index):
        starting_row = (group_index * group_token).astype(jnp.int32)
        query_matrix = lax.dynamic_slice_in_dim(query_row_set, starting_row, group_token, 0).reshape(group_token, KEY_VALUE_HEADS, repeat_factor, HEAD_SIZE)
        key_frame = lax.dynamic_slice_in_dim(key_padding, starting_row, key_span_width, 0).reshape(key_span_width, KEY_VALUE_HEADS, HEAD_SIZE)
        value_frame = lax.dynamic_slice_in_dim(value_padding, starting_row, key_span_width, 0).reshape(key_span_width, KEY_VALUE_HEADS, HEAD_SIZE)
        query_doc = lax.dynamic_slice_in_dim(doc_index, starting_row, group_token, 0)
        key_doc = lax.dynamic_slice_in_dim(doc_pad, starting_row, key_span_width, 0)
        query_pos = starting_row + jnp.arange(group_token, dtype=jnp.int32)
        key_pos = starting_row - leading_padding + jnp.arange(key_span_width, dtype=jnp.int32)
        allowed = (query_doc[:, None] == key_doc[None, :]) & (key_pos[None, :] <= query_pos[:, None]) & (key_pos[None, :] >= 0)
        score_matrix = jnp.einsum("hfwl,afl->fwha", query_matrix.astype(jnp.float32), key_frame.astype(jnp.float32)) * logit_scale
        score_matrix = jnp.where(allowed[None, None], score_matrix, -1e30)
        row_max = jnp.max(score_matrix, -1, keepdims=True)
        exponent = jnp.exp(score_matrix - row_max)
        row_total = jnp.sum(exponent, -1)
        attention_weight = exponent.astype(jnp.bfloat16)
        summed_output = jnp.einsum("mjwh,hmn->mjwn", attention_weight.astype(jnp.float32), value_frame.astype(jnp.float32))
        result = summed_output / row_total[..., None]
        return jnp.transpose(result, (2, 0, 1, 3)).reshape(group_token, QUERY_HEADS * HEAD_SIZE).astype(jnp.bfloat16)

    attended = lax.map(one_group, jnp.arange(groups, dtype=jnp.int32)).reshape(TOKENS, QUERY_HEADS * HEAD_SIZE)
    return attended
```

```python
import math

import jax
import jax.numpy as jnp
from jax import lax
from jax.experimental import pallas as pl
from jax.experimental.pallas import tpu as pltpu
from jax.sharding import PartitionSpec as P

HEAD_SIZE = 128
ROWS = 128
GROUP = 256
WIDTH = 4096
HEADS = 8
KV_HEADS = 2
SHARE = 4
KV = KV_HEADS * HEAD_SIZE
DOC_ROWS = 16
PAY_ROWS = 2 * KV_HEADS * GROUP + DOC_ROWS
Q_ROWS = HEADS * ROWS
DIGIT = 16
NEG = -1e30
SCALE = math.log2(math.e) / math.sqrt(HEAD_SIZE)
F32 = jnp.float32
BF16 = jnp.bfloat16


def dot(a, b):
    return jnp.dot(a, b, preferred_element_type=F32)


def dot_t(a, b):
    return lax.dot_general(a, b, (((1,), (1,)), ((), ())), preferred_element_type=F32)


def own_kv_kernel(own, w_key, w_value, docs, pay, ks, vs, xs, ids, sem, xsem):
    parts = sem.shape[1]
    step = WIDTH // parts
    first = [
        pltpu.make_async_copy(own, xs, xsem.at[0]),
        pltpu.make_async_copy(docs, ids, xsem.at[1]),
    ]
    copies = []
    for i in range(parts):
        cut = pl.ds(i * step, step)
        copies.append(
            [
                pltpu.make_async_copy(w_key.at[cut, :], ks.at[cut, :], sem.at[0, i]),
                pltpu.make_async_copy(w_value.at[cut, :], vs.at[cut, :], sem.at[1, i]),
            ]
        )
    for c in first + sum(copies, []):
        c.start()
    key = jnp.zeros((ROWS, KV), F32)
    value = jnp.zeros((ROWS, KV), F32)
    for c in first:
        c.wait()
    for i in range(parts):
        cut = pl.ds(i * step, step)
        x = xs[:, cut]
        copies[i][0].wait()
        key += dot(x, ks[cut, :])
        copies[i][1].wait()
        value += dot(x, vs[cut, :])
    for j in range(KV_HEADS):
        cols = slice(j * HEAD_SIZE, (j + 1) * HEAD_SIZE)
        pay[j * ROWS : (j + 1) * ROWS, :] = key[:, cols].astype(BF16)
        pay[(KV_HEADS + j) * ROWS : (KV_HEADS + j + 1) * ROWS, :] = value[:, cols].astype(BF16)
    doc = ids[...] + 1
    row = lax.broadcasted_iota(jnp.int32, (DOC_ROWS, ROWS), 0)
    digits = jnp.where(row == 0, doc // DIGIT, jnp.where(row == 1, doc % DIGIT, 0))
    pay[2 * KV_HEADS * ROWS :, :] = digits.astype(F32).astype(BF16)


def other_kv_kernel(other, own_pay, ks, vs, pay):
    x = other[...]
    parts = (dot(x, ks[...]).astype(BF16), dot(x, vs[...]).astype(BF16))
    for j in range(2 * KV_HEADS):
        pay[j * GROUP : j * GROUP + ROWS, :] = own_pay[j * ROWS : (j + 1) * ROWS, :]
        at = (j % KV_HEADS) * HEAD_SIZE
        pay[j * GROUP + ROWS : (j + 1) * GROUP, :] = parts[j // KV_HEADS][:, at : at + HEAD_SIZE]
    pay[2 * KV_HEADS * GROUP :, :] = own_pay[2 * KV_HEADS * ROWS :, :]


def query_kernel(own, other, w_query, pay, q_out, send, xs, ws, acc, sem, xsem):
    parts = sem.shape[0]
    step = WIDTH // parts
    ahead = 2
    x_copies = [
        pltpu.make_async_copy(own, xs.at[pl.ds(0, ROWS), :], xsem.at[0]),
        pltpu.make_async_copy(other, xs.at[pl.ds(ROWS, ROWS), :], xsem.at[1]),
    ]
    copies = []
    for i in range(parts):
        cut = pl.ds(i * step, step)
        copies.append(pltpu.make_async_copy(w_query.at[cut, :], ws.at[cut, :], sem.at[i]))
    for c in x_copies + copies[:ahead]:
        c.start()
    send[Q_ROWS:, :] = pay[...]
    for c in x_copies:
        c.wait()
    for i in range(parts):
        copies[i].wait()
        if i + ahead < parts:
            copies[i + ahead].start()
        cut = pl.ds(i * step, step)
        part = dot(xs[:, cut], ws[cut, :])
        if i == 0:
            acc[...] = part
        elif i < parts - 1:
            acc[...] += part
        else:
            q = (acc[...] + part).astype(BF16)
    for h in range(HEADS):
        rows = slice(h * ROWS, (h + 1) * ROWS)
        q_out[rows, :] = q[:ROWS, rows]
        send[rows, :] = q[ROWS:, rows]


def attend_kernel(q_mine, q_sent, pay, near_mine, near_sent, far_mine, far_sent, out):
    half = lax.axis_index("head")
    base = 2 * KV_HEADS * GROUP

    def ids(ref, start):
        d = ref[start + base : start + base + DOC_ROWS, :].astype(F32)
        return d[0:1] * DIGIT + d[1:2]

    docs = ids(pay, 0)
    doc_q = jnp.transpose(jnp.broadcast_to(docs, (ROWS, ROWS)))
    r = lax.broadcasted_iota(jnp.int32, (ROWS, ROWS), 0)
    c = lax.broadcasted_iota(jnp.int32, (ROWS, ROWS), 1)

    def bias(k):
        return jnp.where(doc_q == k, 0.0, NEG)

    flex_ids = jnp.where(half == 0, ids(far_sent, 0), ids(q_sent, Q_ROWS))
    biases = jnp.concatenate(
        [
            jnp.where((doc_q == docs) & (c <= r), 0.0, NEG),
            bias(ids(near_mine, 0)),
            bias(ids(near_sent, 0)),
            bias(ids(far_mine, 0)),
            bias(flex_ids),
        ],
        axis=1,
    )
    biases = jnp.concatenate([biases] * SHARE, axis=0)
    for side in range(2):
        q_ref = (q_mine, q_sent)[side]
        here, start = ((pay, 0), (q_sent, Q_ROWS))[side]
        near = (near_mine, near_sent)[side]
        far = (far_mine, far_sent)[side]
        mine, other = (0, ROWS) if side == 0 else (ROWS, 0)

        def gather(j):
            at = j * GROUP
            far_other = far[at + other : at + other + ROWS, :]
            here_other = here[start + at + other : start + at + other + ROWS, :]
            return jnp.concatenate(
                [
                    here[start + at + mine : start + at + mine + ROWS, :],
                    near[at + mine : at + mine + ROWS, :],
                    near[at + other : at + other + ROWS, :],
                    far[at + mine : at + mine + ROWS, :],
                    jnp.where(half == 0, far_other, here_other),
                ],
                axis=0,
            )

        for j in range(KV_HEADS):
            k = gather(j)
            v = gather(KV_HEADS + j)
            rows = slice(j * SHARE * ROWS, (j + 1) * SHARE * ROWS)
            s = dot_t(q_ref[rows, :], k) * SCALE + biases
            top = jnp.max(s, axis=1, keepdims=True)
            p = jnp.exp2(s - top)
            total = jnp.sum(p, axis=1, keepdims=True)
            o = (dot(p.astype(BF16), v) / total).astype(BF16)
            for i in range(SHARE):
                place = jnp.where(half == side, 0, HEADS) + j * SHARE + i
                cols = pl.ds(pl.multiple_of(place * HEAD_SIZE, HEAD_SIZE), HEAD_SIZE)
                out[:, cols] = o[i * ROWS : (i + 1) * ROWS, :]


VMEM = pl.BlockSpec(memory_space=pltpu.VMEM)
ANY = pl.BlockSpec(memory_space=pl.ANY)
DMA = pltpu.SemaphoreType.DMA


def call(kernel, name, outs, ins, mib, flops, size, scratch=()):
    many = isinstance(outs, list)
    return pl.pallas_call(
        kernel,
        out_shape=outs,
        in_specs=ins,
        out_specs=[VMEM] * len(outs) if many else VMEM,
        scratch_shapes=list(scratch),
        compiler_params=pltpu.CompilerParams(vmem_limit_bytes=mib << 20),
        cost_estimate=pl.CostEstimate(flops=flops, bytes_accessed=size, transcendentals=0),
        name=name,
    )


def bf16(*shape):
    return pltpu.VMEM(shape, BF16)


def stay(x):
    return pltpu.with_memory_space_constraint(x, pltpu.HBM)


def on_device(tokens, doc_ids, w_query, w_key, value_weight):
    groups = lax.axis_size("srv")

    def swap(x):
        return lax.ppermute(x, "head", [(0, 1), (1, 0)])

    other = swap(tokens)
    parts = 4
    own_pay, ks, vs = call(
        own_kv_kernel,
        "own_kv",
        [bf16(2 * KV_HEADS * ROWS + DOC_ROWS, HEAD_SIZE), bf16(WIDTH, KV), bf16(WIDTH, KV)],
        [ANY] * 4,
        16,
        4 * ROWS * WIDTH * KV,
        5 << 20,
        [
            pltpu.VMEM((ROWS, WIDTH), BF16),
            pltpu.VMEM((1, ROWS), jnp.int32),
            DMA((2, parts)),
            DMA((2,)),
        ],
    )(*map(stay, (tokens, w_key, value_weight, doc_ids.reshape(1, ROWS))))
    pay = call(
        other_kv_kernel,
        "other_kv",
        bf16(PAY_ROWS, HEAD_SIZE),
        [VMEM] * 4,
        16,
        4 * ROWS * WIDTH * KV,
        5 << 20,
    )(other, own_pay, ks, vs)
    near = lax.ppermute(pay, "srv", [(i, i + 1) for i in range(groups - 1)])
    far = lax.ppermute(pay, "srv", [(i, i + 2) for i in range(groups - 2)])
    q_mine, q_send = call(
        query_kernel,
        "query",
        [bf16(Q_ROWS, HEAD_SIZE), bf16(Q_ROWS + PAY_ROWS, HEAD_SIZE)],
        [ANY, ANY, ANY, VMEM],
        24,
        2 * GROUP * WIDTH * HEADS * HEAD_SIZE,
        11 << 20,
        [
            pltpu.VMEM((GROUP, WIDTH), BF16),
            pltpu.VMEM((WIDTH, HEADS * HEAD_SIZE), BF16),
            pltpu.VMEM((GROUP, HEADS * HEAD_SIZE), F32),
            DMA((parts,)),
            DMA((2,)),
        ],
    )(stay(tokens), other, stay(w_query), pay)
    q_sent = swap(q_send)
    near_sent = swap(near)
    far_sent = swap(far)
    return call(
        attend_kernel,
        "attend",
        jax.ShapeDtypeStruct((ROWS, 2 * HEADS * HEAD_SIZE), BF16),
        [VMEM] * 7,
        16,
        4 * ROWS * 5 * ROWS * 2 * HEADS * HEAD_SIZE,
        4 << 20,
    )(q_mine, q_sent, pay, near, near_sent, far, far_sent)


def solution(mesh):
    in_specs = (
        P(("srv", "head"), None),
        P(("srv", "head")),
        P(None, "head"),
        P(None, "head"),
        P(None, "head"),
    )
    out_specs = P(("srv", "head"), None)
    return jax.shard_map(
        on_device, mesh=mesh, in_specs=in_specs, out_specs=out_specs, check_vma=False
    )
```

```python
import math

import jax
import jax.numpy as jnp
from jax import lax
from jax.experimental import pallas as pl
from jax.experimental.pallas import tpu as pltpu
from jax.sharding import PartitionSpec as P

HEAD_SIZE = 128
ROWS = 128
GROUP = 256
WIDTH = 4096
HEADS = 8
KV_HEADS = 2
SHARE = 4
KV = KV_HEADS * HEAD_SIZE
DOC_ROWS = 16
PAY_ROWS = 2 * KV_HEADS * GROUP + DOC_ROWS
Q_ROWS = HEADS * ROWS
DIGIT = 16
NEG = -1e30
SCALE = math.log2(math.e) / math.sqrt(HEAD_SIZE)
F32 = jnp.float32
BF16 = jnp.bfloat16


def dot(a, b):
    return jnp.dot(a, b, preferred_element_type=F32)


def dot_t(a, b):
    return lax.dot_general(a, b, (((1,), (1,)), ((), ())), preferred_element_type=F32)


def first_kernel(out):
    out[...] = jnp.zeros_like(out)


def own_kv_kernel(first, own, w_key, w_value, docs, pay):
    x = own[...]
    key = dot(x, w_key[...])
    value = dot(x, w_value[...])
    for j in range(KV_HEADS):
        cols = slice(j * HEAD_SIZE, (j + 1) * HEAD_SIZE)
        pay[j * ROWS : (j + 1) * ROWS, :] = key[:, cols].astype(BF16)
        pay[(KV_HEADS + j) * ROWS : (KV_HEADS + j + 1) * ROWS, :] = value[:, cols].astype(BF16)
    doc = docs[...] + 1
    row = lax.broadcasted_iota(jnp.int32, (DOC_ROWS, ROWS), 0)
    digits = jnp.where(row == 0, doc // DIGIT, jnp.where(row == 1, doc % DIGIT, 0))
    pay[2 * KV_HEADS * ROWS :, :] = digits.astype(F32).astype(BF16)


def other_kv_kernel(other, own_pay, ks, vs, pay):
    x = other[...]
    parts = (dot(x, ks[...]).astype(BF16), dot(x, vs[...]).astype(BF16))
    for j in range(2 * KV_HEADS):
        pay[j * GROUP : j * GROUP + ROWS, :] = own_pay[j * ROWS : (j + 1) * ROWS, :]
        at = (j % KV_HEADS) * HEAD_SIZE
        pay[j * GROUP + ROWS : (j + 1) * GROUP, :] = parts[j // KV_HEADS][:, at : at + HEAD_SIZE]
    pay[2 * KV_HEADS * GROUP :, :] = own_pay[2 * KV_HEADS * ROWS :, :]


def query_kernel(own, other, w_query, pay, q_out, send):
    step = 2 * HEAD_SIZE
    send[Q_ROWS:, :] = pay[...]
    for i in range(HEADS // 2):
        w = w_query[:, i * step : (i + 1) * step]
        mine = dot(own[...], w).astype(BF16)
        theirs = dot(other[...], w).astype(BF16)
        for j in range(2):
            rows = pl.ds((2 * i + j) * ROWS, ROWS)
            cols = slice(j * HEAD_SIZE, (j + 1) * HEAD_SIZE)
            q_out[rows, :] = mine[:, cols]
            send[rows, :] = theirs[:, cols]


BASE = 2 * KV_HEADS * GROUP


def ids_of(ref, start=0):
    d = ref[start + BASE : start + BASE + DOC_ROWS, :].astype(F32)
    return d[0:1] * DIGIT + d[1:2]


def down(ids):
    return jnp.transpose(jnp.broadcast_to(ids, (ROWS, ROWS)))


def tall(*blocks):
    return jnp.concatenate([jnp.concatenate(blocks, axis=1)] * SHARE, axis=0)


def wide(x):
    return jnp.broadcast_to(x, (SHARE * ROWS, HEAD_SIZE))


def near_kernel(q_mine, q_sent, pay, near_mine, near_sent, acc_out, m_out, l_out):
    half = lax.axis_index("head")
    docs = ids_of(pay)
    doc_q = down(docs)
    r = lax.broadcasted_iota(jnp.int32, (ROWS, ROWS), 0)
    c = lax.broadcasted_iota(jnp.int32, (ROWS, ROWS), 1)
    here_mine = jnp.where((doc_q == docs) & (c <= r), 0.0, NEG)
    here_other = jnp.where((doc_q == ids_of(q_sent, Q_ROWS)) & (c < half * ROWS), 0.0, NEG)
    near_a = jnp.where(doc_q == ids_of(near_mine), 0.0, NEG)
    near_b = jnp.where(doc_q == ids_of(near_sent), 0.0, NEG)
    for side in range(2):
        if side == 0:
            q_ref, here, start, near = q_mine, pay, 0, near_mine
            bias = tall(here_mine, here_other, near_a, near_b)
        else:
            q_ref, here, start, near = q_sent, q_sent, Q_ROWS, near_sent
            bias = tall(here_other, here_mine, near_b, near_a)
        for j in range(KV_HEADS):
            rows = pl.ds(j * SHARE * ROWS, SHARE * ROWS)
            k_at = j * GROUP
            v_at = (KV_HEADS + j) * GROUP
            k = jnp.concatenate([here[pl.ds(start + k_at, GROUP), :], near[pl.ds(k_at, GROUP), :]], axis=0)
            v = jnp.concatenate([here[pl.ds(start + v_at, GROUP), :], near[pl.ds(v_at, GROUP), :]], axis=0)
            s = dot_t(q_ref[rows, :], k) * SCALE + bias
            top = jnp.max(s, axis=1, keepdims=True)
            p = jnp.exp2(s - top)
            to = pl.ds((side * HEADS + j * SHARE) * ROWS, SHARE * ROWS)
            m_out[to, :] = wide(top)
            l_out[to, :] = wide(jnp.sum(p, axis=1, keepdims=True))
            acc_out[to, :] = dot(p.astype(BF16), v)


def far_kernel(q_mine, q_sent, pay, far_mine, far_sent, acc_in, m_in, l_in, out, buf, sem):
    half = lax.axis_index("head")
    doc_q = down(ids_of(pay))
    far_a = jnp.where(doc_q == ids_of(far_mine), 0.0, NEG)
    far_b = jnp.where(doc_q == ids_of(far_sent), 0.0, NEG)
    copies = []
    for side in range(2):
        q_ref = (q_mine, q_sent)[side]
        far = (far_mine, far_sent)[side]
        bias = tall(far_a, far_b) if side == 0 else tall(far_b, far_a)
        for j in range(KV_HEADS):
            rows = pl.ds(j * SHARE * ROWS, SHARE * ROWS)
            at = pl.ds((side * HEADS + j * SHARE) * ROWS, SHARE * ROWS)
            s = dot_t(q_ref[rows, :], far[pl.ds(j * GROUP, GROUP), :]) * SCALE + bias
            old = m_in[at, :]
            top = jnp.maximum(old, wide(jnp.max(s, axis=1, keepdims=True)))
            factor = jnp.exp2(old - top)
            p = jnp.exp2(s - jnp.concatenate([top, top], axis=1))
            total = l_in[at, :] * factor + wide(jnp.sum(p, axis=1, keepdims=True))
            acc = acc_in[at, :] * factor
            acc += dot(p.astype(BF16), far[pl.ds((KV_HEADS + j) * GROUP, GROUP), :])
            o = (acc / total).astype(BF16)
            for i in range(SHARE):
                col = (j * SHARE + i) * HEAD_SIZE
                buf[side, :, col : col + HEAD_SIZE] = o[i * ROWS : (i + 1) * ROWS, :]
        width = HEADS * HEAD_SIZE
        start = pl.multiple_of(jnp.where(half == side, 0, width), width)
        copy = pltpu.make_async_copy(buf.at[side], out.at[:, pl.ds(start, width)], sem.at[side])
        copy.start()
        copies.append(copy)
    for copy in copies:
        copy.wait()


VMEM = pl.BlockSpec(memory_space=pltpu.VMEM)
ANY = pl.BlockSpec(memory_space=pl.ANY)
DMA = pltpu.SemaphoreType.DMA


def call(kernel, name, outs, ins, mib, flops, size, scratch=(), to=None):
    many = isinstance(outs, list)
    return pl.pallas_call(
        kernel,
        out_shape=outs,
        in_specs=ins,
        out_specs=[VMEM] * len(outs) if many else to or VMEM,
        scratch_shapes=list(scratch),
        compiler_params=pltpu.CompilerParams(vmem_limit_bytes=mib << 20),
        cost_estimate=pl.CostEstimate(flops=flops, bytes_accessed=size, transcendentals=0),
        name=name,
    )


def bf16(*shape):
    return pltpu.VMEM(shape, BF16)


def fast(x):
    return pltpu.with_memory_space_constraint(x, pltpu.VMEM)


def on_device(tokens, doc_ids, w_query, w_key, value_weight):
    groups = lax.axis_size("srv")

    def swap(x):
        return lax.ppermute(x, "head", [(0, 1), (1, 0)])

    first = call(first_kernel, "first", bf16(DOC_ROWS, HEAD_SIZE), [], 1, 10**11, 10**11)()
    own, w_query, w_key, w_value = map(fast, (tokens, w_query, w_key, value_weight))
    other = swap(tokens)
    flops = 4 * ROWS * WIDTH * KV
    own_pay = call(
        own_kv_kernel,
        "own_kv",
        bf16(2 * KV_HEADS * ROWS + DOC_ROWS, HEAD_SIZE),
        [ANY] + [VMEM] * 4,
        16,
        flops,
        5 << 20,
    )(first, own, w_key, w_value, doc_ids.reshape(1, ROWS))
    pay = call(
        other_kv_kernel, "other_kv", bf16(PAY_ROWS, HEAD_SIZE), [VMEM] * 4, 16, flops, 5 << 20
    )(other, own_pay, w_key, w_value)
    near = lax.ppermute(pay, "srv", [(i, i + 1) for i in range(groups - 1)])
    far = lax.ppermute(pay, "srv", [(i, i + 2) for i in range(groups - 2)])
    q_mine, q_send = call(
        query_kernel,
        "query",
        [bf16(Q_ROWS, HEAD_SIZE), bf16(Q_ROWS + PAY_ROWS, HEAD_SIZE)],
        [VMEM] * 4,
        24,
        2 * GROUP * WIDTH * HEADS * HEAD_SIZE,
        11 << 20,
    )(own, other, w_query, pay)
    q_sent = swap(q_send)
    near_sent = swap(near)
    far_sent = swap(far)
    pairs = ROWS * GROUP * 2 * HEADS * HEAD_SIZE
    acc, m, l = call(
        near_kernel,
        "attend_near",
        [pltpu.VMEM((2 * Q_ROWS, n), F32) for n in [HEAD_SIZE] * 3],
        [VMEM] * 5,
        16,
        1,
        1,
    )(q_mine, q_sent, pay, near, near_sent)
    return call(
        far_kernel,
        "attend_far",
        jax.ShapeDtypeStruct((ROWS, 2 * HEADS * HEAD_SIZE), BF16),
        [VMEM] * 8,
        16,
        4 * pairs,
        4 << 20,
        [pltpu.VMEM((2, ROWS, HEADS * HEAD_SIZE), BF16), DMA((2,))],
        ANY,
    )(q_mine, q_sent, pay, far, far_sent, acc, m, l)


def solution(mesh):
    in_specs = (
        P(("srv", "head"), None),
        P(("srv", "head")),
        P(None, "head"),
        P(None, "head"),
        P(None, "head"),
    )
    out_specs = P(("srv", "head"), None)
    return jax.shard_map(
        on_device, mesh=mesh, in_specs=in_specs, out_specs=out_specs, check_vma=False
    )
```

```python
import math

import jax
import jax.numpy as jnp
from jax import lax
from jax.experimental import pallas as pl
from jax.experimental.pallas import tpu as pltpu
from jax.sharding import PartitionSpec as P

HEAD_SIZE = 128
ROWS = 128
GROUP = 256
WIDTH = 4096
HEADS = 8
KV_HEADS = 2
SHARE = 4
KV = KV_HEADS * HEAD_SIZE
DOC_ROWS = 16
PAY_ROWS = 2 * KV_HEADS * GROUP + DOC_ROWS
Q_ROWS = HEADS * ROWS
DIGIT = 16
NEG = -1e30
SCALE = math.log2(math.e) / math.sqrt(HEAD_SIZE)
F32 = jnp.float32
BF16 = jnp.bfloat16


def dot(a, b):
    return jnp.dot(a, b, preferred_element_type=F32)


def dot_t(a, b):
    return lax.dot_general(a, b, (((1,), (1,)), ((), ())), preferred_element_type=F32)


def first_kernel(out):
    out[...] = jnp.zeros_like(out)


def own_kv_kernel(first, own, w_key, w_value, docs, pay):
    x = own[...]
    key = dot(x, w_key[...])
    value = dot(x, w_value[...])
    for j in range(KV_HEADS):
        cols = slice(j * HEAD_SIZE, (j + 1) * HEAD_SIZE)
        pay[j * ROWS : (j + 1) * ROWS, :] = key[:, cols].astype(BF16)
        pay[(KV_HEADS + j) * ROWS : (KV_HEADS + j + 1) * ROWS, :] = value[:, cols].astype(BF16)
    doc = docs[...] + 1
    row = lax.broadcasted_iota(jnp.int32, (DOC_ROWS, ROWS), 0)
    digits = jnp.where(row == 0, doc // DIGIT, jnp.where(row == 1, doc % DIGIT, 0))
    pay[2 * KV_HEADS * ROWS :, :] = digits.astype(F32).astype(BF16)


def other_kv_kernel(other, own_pay, ks, vs, pay):
    x = other[...]
    parts = (dot(x, ks[...]).astype(BF16), dot(x, vs[...]).astype(BF16))
    for j in range(2 * KV_HEADS):
        pay[j * GROUP : j * GROUP + ROWS, :] = own_pay[j * ROWS : (j + 1) * ROWS, :]
        at = (j % KV_HEADS) * HEAD_SIZE
        pay[j * GROUP + ROWS : (j + 1) * GROUP, :] = parts[j // KV_HEADS][:, at : at + HEAD_SIZE]
    pay[2 * KV_HEADS * GROUP :, :] = own_pay[2 * KV_HEADS * ROWS :, :]


def query_kernel(own, other, w_query, pay, q_out, send):
    step = 2 * HEAD_SIZE
    send[Q_ROWS:, :] = pay[...]
    for i in range(HEADS // 2):
        w = w_query[:, i * step : (i + 1) * step]
        mine = dot(own[...], w).astype(BF16)
        theirs = dot(other[...], w).astype(BF16)
        for j in range(2):
            rows = pl.ds((2 * i + j) * ROWS, ROWS)
            cols = slice(j * HEAD_SIZE, (j + 1) * HEAD_SIZE)
            q_out[rows, :] = mine[:, cols]
            send[rows, :] = theirs[:, cols]


BASE = 2 * KV_HEADS * GROUP


def ids_of(ref, start=0):
    d = ref[start + BASE : start + BASE + DOC_ROWS, :].astype(F32)
    return d[0:1] * DIGIT + d[1:2]


def down(ids):
    return jnp.transpose(jnp.broadcast_to(ids, (ROWS, ROWS)))


def tall(*blocks):
    return jnp.concatenate([jnp.concatenate(blocks, axis=1)] * SHARE, axis=0)


def wide(x):
    return jnp.broadcast_to(x, (SHARE * ROWS, HEAD_SIZE))


def place(o, side, j, buf):
    for i in range(SHARE):
        col = (j * SHARE + i) * HEAD_SIZE
        buf[side, :, col : col + HEAD_SIZE] = o[i * ROWS : (i + 1) * ROWS, :]


def side_copy(buf, out, sem, side, j):
    width = SHARE * HEAD_SIZE
    start = jnp.where(lax.axis_index("head") == side, 0, HEADS * HEAD_SIZE) + j * width
    to = out.at[:, pl.ds(pl.multiple_of(start, width), width)]
    return pltpu.make_async_copy(buf.at[side, :, pl.ds(j * width, width)], to, sem.at[side, j])


def wait_all(buf, out, sem):
    for side in range(2):
        for j in range(KV_HEADS):
            side_copy(buf, out, sem, side, j).wait()


def near_kernel(q_mine, q_sent, pay, near_mine, near_sent, out, acc_out, m_out, l_out, buf, sem):
    half = lax.axis_index("head")
    docs = ids_of(pay)
    doc_q = down(docs)
    r = lax.broadcasted_iota(jnp.int32, (ROWS, ROWS), 0)
    c = lax.broadcasted_iota(jnp.int32, (ROWS, ROWS), 1)
    here_mine = jnp.where((doc_q == docs) & (c <= r), 0.0, NEG)
    here_other = jnp.where((doc_q == ids_of(q_sent, Q_ROWS)) & (c < half * ROWS), 0.0, NEG)
    near_a = jnp.where(doc_q == ids_of(near_mine), 0.0, NEG)
    near_b = jnp.where(doc_q == ids_of(near_sent), 0.0, NEG)
    for side in range(2):
        if side == 0:
            q_ref, here, start, near = q_mine, pay, 0, near_mine
            bias = tall(here_mine, here_other, near_a, near_b)
        else:
            q_ref, here, start, near = q_sent, q_sent, Q_ROWS, near_sent
            bias = tall(here_other, here_mine, near_b, near_a)
        for j in range(KV_HEADS):
            rows = pl.ds(j * SHARE * ROWS, SHARE * ROWS)
            k_at = j * GROUP
            v_at = (KV_HEADS + j) * GROUP
            k = jnp.concatenate([here[pl.ds(start + k_at, GROUP), :], near[pl.ds(k_at, GROUP), :]], axis=0)
            v = jnp.concatenate([here[pl.ds(start + v_at, GROUP), :], near[pl.ds(v_at, GROUP), :]], axis=0)
            s = dot_t(q_ref[rows, :], k) * SCALE + bias
            top = jnp.max(s, axis=1, keepdims=True)
            p = jnp.exp2(s - top)
            to = pl.ds((side * HEADS + j * SHARE) * ROWS, SHARE * ROWS)
            total = jnp.sum(p, axis=1, keepdims=True)
            acc = dot(p.astype(BF16), v)
            m_out[to, :] = wide(top)
            l_out[to, :] = wide(total)
            acc_out[to, :] = acc
            place((acc / total).astype(BF16), side, j, buf)
            side_copy(buf, out, sem, side, j).start()
    wait_all(buf, out, sem)


def far_kernel(q_mine, q_sent, pay, far_mine, far_sent, acc_in, m_in, l_in, before, out, buf, sem):
    half = lax.axis_index("head")
    docs = ids_of(pay)
    docs_a = ids_of(far_mine)
    docs_b = ids_of(far_sent)
    last = jnp.max(jnp.where(half == 0, docs_b, docs_a))

    @pl.when(last == jnp.min(docs))
    def _():
        doc_q = down(docs)
        far_a = jnp.where(doc_q == docs_a, 0.0, NEG)
        far_b = jnp.where(doc_q == docs_b, 0.0, NEG)
        for side in range(2):
            q_ref = (q_mine, q_sent)[side]
            far = (far_mine, far_sent)[side]
            bias = tall(far_a, far_b) if side == 0 else tall(far_b, far_a)
            for j in range(KV_HEADS):
                rows = pl.ds(j * SHARE * ROWS, SHARE * ROWS)
                at = pl.ds((side * HEADS + j * SHARE) * ROWS, SHARE * ROWS)
                s = dot_t(q_ref[rows, :], far[pl.ds(j * GROUP, GROUP), :]) * SCALE + bias
                old = m_in[at, :]
                top = jnp.maximum(old, wide(jnp.max(s, axis=1, keepdims=True)))
                factor = jnp.exp2(old - top)
                p = jnp.exp2(s - jnp.concatenate([top, top], axis=1))
                total = l_in[at, :] * factor + wide(jnp.sum(p, axis=1, keepdims=True))
                acc = acc_in[at, :] * factor
                acc += dot(p.astype(BF16), far[pl.ds((KV_HEADS + j) * GROUP, GROUP), :])
                place((acc / total).astype(BF16), side, j, buf)
                side_copy(buf, out, sem, side, j).start()
        wait_all(buf, out, sem)


VMEM = pl.BlockSpec(memory_space=pltpu.VMEM)
ANY = pl.BlockSpec(memory_space=pl.ANY)
DMA = pltpu.SemaphoreType.DMA


def call(kernel, name, outs, ins, mib, flops, size, scratch=(), to=None, alias={}):
    many = isinstance(outs, list)
    return pl.pallas_call(
        kernel,
        out_shape=outs,
        in_specs=ins,
        out_specs=to or ([VMEM] * len(outs) if many else VMEM),
        input_output_aliases=alias,
        scratch_shapes=list(scratch),
        compiler_params=pltpu.CompilerParams(vmem_limit_bytes=mib << 20),
        cost_estimate=pl.CostEstimate(flops=flops, bytes_accessed=size, transcendentals=0),
        name=name,
    )


def bf16(*shape):
    return pltpu.VMEM(shape, BF16)


def fast(x):
    return pltpu.with_memory_space_constraint(x, pltpu.VMEM)


def on_device(tokens, doc_ids, w_query, w_key, value_weight):
    groups = lax.axis_size("srv")

    def swap(x):
        return lax.ppermute(x, "head", [(0, 1), (1, 0)])

    first = call(first_kernel, "first", bf16(DOC_ROWS, HEAD_SIZE), [], 1, 10**11, 10**11)()
    own, w_query, w_key, w_value = map(fast, (tokens, w_query, w_key, value_weight))
    other = swap(tokens)
    flops = 4 * ROWS * WIDTH * KV
    own_pay = call(
        own_kv_kernel,
        "own_kv",
        bf16(2 * KV_HEADS * ROWS + DOC_ROWS, HEAD_SIZE),
        [ANY] + [VMEM] * 4,
        16,
        flops,
        5 << 20,
    )(first, own, w_key, w_value, doc_ids.reshape(1, ROWS))
    pay = call(
        other_kv_kernel, "other_kv", bf16(PAY_ROWS, HEAD_SIZE), [VMEM] * 4, 16, flops, 5 << 20
    )(other, own_pay, w_key, w_value)
    near = lax.ppermute(pay, "srv", [(i, i + 1) for i in range(groups - 1)])
    far = lax.ppermute(pay, "srv", [(i, i + 2) for i in range(groups - 2)])
    q_mine, q_send = call(
        query_kernel,
        "query",
        [bf16(Q_ROWS, HEAD_SIZE), bf16(Q_ROWS + PAY_ROWS, HEAD_SIZE)],
        [VMEM] * 4,
        24,
        2 * GROUP * WIDTH * HEADS * HEAD_SIZE,
        11 << 20,
    )(own, other, w_query, pay)
    q_sent = swap(q_send)
    near_sent = swap(near)
    far_sent = swap(far)
    pairs = ROWS * GROUP * 2 * HEADS * HEAD_SIZE
    result = jax.ShapeDtypeStruct((ROWS, 2 * HEADS * HEAD_SIZE), BF16)
    sides = [pltpu.VMEM((2, ROWS, HEADS * HEAD_SIZE), BF16), DMA((2, KV_HEADS))]
    out, acc, m, l = call(
        near_kernel,
        "attend_near",
        [result] + [pltpu.VMEM((2 * Q_ROWS, HEAD_SIZE), F32)] * 3,
        [VMEM] * 5,
        16,
        1,
        1,
        sides,
        [ANY] + [VMEM] * 3,
    )(q_mine, q_sent, pay, near, near_sent)
    return call(
        far_kernel,
        "attend_far",
        result,
        [VMEM] * 8 + [ANY],
        16,
        4 * pairs,
        4 << 20,
        sides,
        ANY,
        {8: 0},
    )(q_mine, q_sent, pay, far, far_sent, acc, m, l, out)


def solution(mesh):
    in_specs = (
        P(("srv", "head"), None),
        P(("srv", "head")),
        P(None, "head"),
        P(None, "head"),
        P(None, "head"),
    )
    out_specs = P(("srv", "head"), None)
    return jax.shard_map(
        on_device, mesh=mesh, in_specs=in_specs, out_specs=out_specs, check_vma=False
    )
```

```python
import math

import jax
import jax.numpy as jnp
from jax import lax
from jax.experimental import pallas as pl
from jax.experimental.pallas import tpu as pltpu
from jax.sharding import PartitionSpec as P

HEAD_SIZE = 128
ROWS = 128
GROUP = 256
WIDTH = 4096
HEADS = 8
KV_HEADS = 2
SHARE = 4
KV = KV_HEADS * HEAD_SIZE
DOC_ROWS = 16
PAY_ROWS = 2 * KV_HEADS * GROUP + DOC_ROWS
Q_ROWS = HEADS * ROWS
DIGIT = 16
NEG = -1e30
SCALE = math.log2(math.e) / math.sqrt(HEAD_SIZE)
F32 = jnp.float32
BF16 = jnp.bfloat16


def dot(a, b):
    return jnp.dot(a, b, preferred_element_type=F32)


def dot_t(a, b):
    return lax.dot_general(a, b, (((1,), (1,)), ((), ())), preferred_element_type=F32)


def first_kernel(out):
    out[...] = jnp.zeros_like(out)


def own_kv_kernel(first, own, w_key, w_value, docs, pay):
    x = own[...]
    key = dot(x, w_key[...])
    value = dot(x, w_value[...])
    for j in range(KV_HEADS):
        cols = slice(j * HEAD_SIZE, (j + 1) * HEAD_SIZE)
        pay[j * ROWS : (j + 1) * ROWS, :] = key[:, cols].astype(BF16)
        pay[(KV_HEADS + j) * ROWS : (KV_HEADS + j + 1) * ROWS, :] = value[:, cols].astype(BF16)
    doc = docs[...] + 1
    row = lax.broadcasted_iota(jnp.int32, (DOC_ROWS, ROWS), 0)
    digits = jnp.where(row == 0, doc // DIGIT, jnp.where(row == 1, doc % DIGIT, 0))
    pay[2 * KV_HEADS * ROWS :, :] = digits.astype(F32).astype(BF16)


def other_kv_kernel(other, own_pay, ks, vs, pay):
    x = other[...]
    parts = (dot(x, ks[...]).astype(BF16), dot(x, vs[...]).astype(BF16))
    for j in range(2 * KV_HEADS):
        pay[j * GROUP : j * GROUP + ROWS, :] = own_pay[j * ROWS : (j + 1) * ROWS, :]
        at = (j % KV_HEADS) * HEAD_SIZE
        pay[j * GROUP + ROWS : (j + 1) * GROUP, :] = parts[j // KV_HEADS][:, at : at + HEAD_SIZE]
    pay[2 * KV_HEADS * GROUP :, :] = own_pay[2 * KV_HEADS * ROWS :, :]


def query_kernel(own, other, w_query, pay, q_out, send):
    step = 2 * HEAD_SIZE
    send[Q_ROWS:, :] = pay[...]
    for i in range(HEADS // 2):
        w = w_query[:, i * step : (i + 1) * step]
        mine = dot(own[...], w).astype(BF16)
        theirs = dot(other[...], w).astype(BF16)
        for j in range(2):
            rows = pl.ds((2 * i + j) * ROWS, ROWS)
            cols = slice(j * HEAD_SIZE, (j + 1) * HEAD_SIZE)
            q_out[rows, :] = mine[:, cols]
            send[rows, :] = theirs[:, cols]


BASE = 2 * KV_HEADS * GROUP


def ids_of(ref, start=0):
    d = ref[start + BASE : start + BASE + DOC_ROWS, :].astype(F32)
    return d[0:1] * DIGIT + d[1:2]


def down(ids):
    return jnp.transpose(jnp.broadcast_to(ids, (ROWS, ROWS)))


def scores(q, k, bias):
    s = dot_t(q, k).reshape(SHARE, ROWS, k.shape[0]) * SCALE + bias[None]
    return s.reshape(SHARE * ROWS, k.shape[0])


def side_by_side(*blocks):
    return jnp.concatenate(blocks, axis=1)


def wide(x):
    return jnp.broadcast_to(x, (SHARE * ROWS, HEAD_SIZE))


def place(o, side, j, buf):
    for i in range(SHARE):
        col = (j * SHARE + i) * HEAD_SIZE
        buf[side, :, col : col + HEAD_SIZE] = o[i * ROWS : (i + 1) * ROWS, :]


def side_copy(buf, out, sem, side, j):
    width = SHARE * HEAD_SIZE
    start = jnp.where(lax.axis_index("head") == side, 0, HEADS * HEAD_SIZE) + j * width
    to = out.at[:, pl.ds(pl.multiple_of(start, width), width)]
    return pltpu.make_async_copy(buf.at[side, :, pl.ds(j * width, width)], to, sem.at[side, j])


def wait_all(buf, out, sem):
    for side in range(2):
        for j in range(KV_HEADS):
            side_copy(buf, out, sem, side, j).wait()


def near_kernel(q_mine, q_sent, pay, near_mine, near_sent, out, acc_out, m_out, l_out, flag, buf, sem):
    half = lax.axis_index("head")
    docs = ids_of(pay)
    doc_q = down(docs)
    r = lax.broadcasted_iota(jnp.int32, (ROWS, ROWS), 0)
    c = lax.broadcasted_iota(jnp.int32, (ROWS, ROWS), 1)
    here_a = jnp.where((doc_q == docs) & (c <= r), 0.0, NEG)
    here_b = jnp.where((doc_q == ids_of(q_sent, Q_ROWS)) & (c < half * ROWS), 0.0, NEG)
    near_a = jnp.where(doc_q == ids_of(near_mine), 0.0, NEG)
    near_b = jnp.where(doc_q == ids_of(near_sent), 0.0, NEG)

    def attend(final):
        for side in range(2):
            if side == 0:
                q_ref, here, start, near = q_mine, pay, 0, near_mine
                bias = side_by_side(here_a, here_b, near_a, near_b)
            else:
                q_ref, here, start, near = q_sent, q_sent, Q_ROWS, near_sent
                bias = side_by_side(here_b, here_a, near_b, near_a)

            def gather(j):
                at = j * GROUP
                return jnp.concatenate([here[pl.ds(start + at, GROUP), :], near[pl.ds(at, GROUP), :]], axis=0)

            for j in range(KV_HEADS):
                rows = pl.ds(j * SHARE * ROWS, SHARE * ROWS)
                s = scores(q_ref[rows, :], gather(j), bias)
                top = jnp.max(s, axis=1, keepdims=True)
                p = jnp.exp2(s - top)
                total = jnp.sum(p, axis=1, keepdims=True)
                acc = dot(p.astype(BF16), gather(KV_HEADS + j))
                if final:
                    place((acc / total).astype(BF16), side, j, buf)
                    side_copy(buf, out, sem, side, j).start()
                else:
                    to = pl.ds((side * HEADS + j * SHARE) * ROWS, SHARE * ROWS)
                    m_out[to, :] = wide(top)
                    l_out[to, :] = wide(total)
                    acc_out[to, :] = acc
        if final:
            wait_all(buf, out, sem)

    first = jnp.where(half == 0, ids_of(near_mine), ids_of(near_sent))
    more = jnp.min(first) == jnp.min(docs)
    flag[...] = jnp.where(more, 1.0, 0.0) * jnp.ones_like(flag)

    @pl.when(more)
    def _():
        attend(False)

    @pl.when(jnp.logical_not(more))
    def _():
        attend(True)


def far_kernel(q_mine, q_sent, pay, far_mine, far_sent, acc_in, m_in, l_in, flag, before, out, buf, sem):
    @pl.when(jnp.max(flag[...]) > 0.5)
    def _():
        doc_q = down(ids_of(pay))
        far_a = jnp.where(doc_q == ids_of(far_mine), 0.0, NEG)
        far_b = jnp.where(doc_q == ids_of(far_sent), 0.0, NEG)
        for side in range(2):
            q_ref = (q_mine, q_sent)[side]
            far = (far_mine, far_sent)[side]
            bias = side_by_side(far_a, far_b) if side == 0 else side_by_side(far_b, far_a)
            for j in range(KV_HEADS):
                rows = pl.ds(j * SHARE * ROWS, SHARE * ROWS)
                at = pl.ds((side * HEADS + j * SHARE) * ROWS, SHARE * ROWS)
                s = scores(q_ref[rows, :], far[pl.ds(j * GROUP, GROUP), :], bias)
                old = m_in[at, :]
                top = jnp.maximum(old, wide(jnp.max(s, axis=1, keepdims=True)))
                factor = jnp.exp2(old - top)
                p = jnp.exp2(s - jnp.concatenate([top, top], axis=1))
                total = l_in[at, :] * factor + wide(jnp.sum(p, axis=1, keepdims=True))
                acc = acc_in[at, :] * factor
                acc += dot(p.astype(BF16), far[pl.ds((KV_HEADS + j) * GROUP, GROUP), :])
                place((acc / total).astype(BF16), side, j, buf)
                side_copy(buf, out, sem, side, j).start()
        wait_all(buf, out, sem)


VMEM = pl.BlockSpec(memory_space=pltpu.VMEM)
ANY = pl.BlockSpec(memory_space=pl.ANY)
DMA = pltpu.SemaphoreType.DMA


def call(kernel, name, outs, ins, mib, flops, size, scratch=(), to=None, alias={}):
    many = isinstance(outs, list)
    return pl.pallas_call(
        kernel,
        out_shape=outs,
        in_specs=ins,
        out_specs=to or ([VMEM] * len(outs) if many else VMEM),
        input_output_aliases=alias,
        scratch_shapes=list(scratch),
        compiler_params=pltpu.CompilerParams(vmem_limit_bytes=mib << 20),
        cost_estimate=pl.CostEstimate(flops=flops, bytes_accessed=size, transcendentals=0),
        name=name,
    )


def bf16(*shape):
    return pltpu.VMEM(shape, BF16)


def fast(x):
    return pltpu.with_memory_space_constraint(x, pltpu.VMEM)


def on_device(tokens, doc_ids, w_query, w_key, value_weight):
    groups = lax.axis_size("srv")

    def swap(x):
        return lax.ppermute(x, "head", [(0, 1), (1, 0)])

    first = call(first_kernel, "first", bf16(DOC_ROWS, HEAD_SIZE), [], 1, 10**11, 10**11)()
    own, w_query, w_key, w_value = map(fast, (tokens, w_query, w_key, value_weight))
    other = swap(tokens)
    flops = 4 * ROWS * WIDTH * KV
    own_pay = call(
        own_kv_kernel,
        "own_kv",
        bf16(2 * KV_HEADS * ROWS + DOC_ROWS, HEAD_SIZE),
        [ANY] + [VMEM] * 4,
        16,
        flops,
        5 << 20,
    )(first, own, w_key, w_value, doc_ids.reshape(1, ROWS))
    pay = call(
        other_kv_kernel, "other_kv", bf16(PAY_ROWS, HEAD_SIZE), [VMEM] * 4, 16, flops, 5 << 20
    )(other, own_pay, w_key, w_value)
    near = lax.ppermute(pay, "srv", [(i, i + 1) for i in range(groups - 1)])
    far = lax.ppermute(pay, "srv", [(i, i + 2) for i in range(groups - 2)])
    q_mine, q_send = call(
        query_kernel,
        "query",
        [bf16(Q_ROWS, HEAD_SIZE), bf16(Q_ROWS + PAY_ROWS, HEAD_SIZE)],
        [VMEM] * 4,
        24,
        2 * GROUP * WIDTH * HEADS * HEAD_SIZE,
        11 << 20,
    )(own, other, w_query, pay)
    q_sent = swap(q_send)
    near_sent = swap(near)
    far_sent = swap(far)
    pairs = ROWS * GROUP * 2 * HEADS * HEAD_SIZE
    result = jax.ShapeDtypeStruct((ROWS, 2 * HEADS * HEAD_SIZE), BF16)
    sides = [pltpu.VMEM((2, ROWS, HEADS * HEAD_SIZE), BF16), DMA((2, KV_HEADS))]
    out, acc, m, l, flag = call(
        near_kernel,
        "attend_near",
        [result] + [pltpu.VMEM((2 * Q_ROWS, HEAD_SIZE), F32)] * 3 + [pltpu.VMEM((8, HEAD_SIZE), F32)],
        [VMEM] * 5,
        16,
        1,
        1,
        sides,
        [ANY] + [VMEM] * 4,
    )(q_mine, q_sent, pay, near, near_sent)
    return call(
        far_kernel,
        "attend_far",
        result,
        [VMEM] * 9 + [ANY],
        16,
        4 * pairs,
        4 << 20,
        sides,
        ANY,
        {9: 0},
    )(q_mine, q_sent, pay, far, far_sent, acc, m, l, flag, out)


def solution(mesh):
    in_specs = (
        P(("srv", "head"), None),
        P(("srv", "head")),
        P(None, "head"),
        P(None, "head"),
        P(None, "head"),
    )
    out_specs = P(("srv", "head"), None)
    return jax.shard_map(
        on_device, mesh=mesh, in_specs=in_specs, out_specs=out_specs, check_vma=False
    )
```

```python
import math

import jax
import jax.numpy as jnp
from jax import lax
from jax.experimental import pallas as pl
from jax.experimental.pallas import tpu as pltpu
from jax.sharding import PartitionSpec as P

HEAD_SIZE = 128
ROWS = 128
GROUP = 256
WIDTH = 4096
HEADS = 8
KV_HEADS = 2
SHARE = 4
KV = KV_HEADS * HEAD_SIZE
DOC_ROWS = 16
PAY_ROWS = 2 * KV_HEADS * GROUP + DOC_ROWS
Q_ROWS = HEADS * ROWS
DIGIT = 16
NEG = -1e30
SCALE = math.log2(math.e) / math.sqrt(HEAD_SIZE)
F32 = jnp.float32
BF16 = jnp.bfloat16


def dot(a, b):
    return jnp.dot(a, b, preferred_element_type=F32)


def dot_t(a, b):
    return lax.dot_general(a, b, (((1,), (1,)), ((), ())), preferred_element_type=F32)


def first_kernel(*refs):
    out = refs[-1]
    out[...] = jnp.zeros_like(out)


def own_kv_kernel(first, own, w_key, w_value, docs, pay):
    x = own[...]
    key = dot(x, w_key[...])
    value = dot(x, w_value[...])
    for j in range(KV_HEADS):
        cols = slice(j * HEAD_SIZE, (j + 1) * HEAD_SIZE)
        pay[j * ROWS : (j + 1) * ROWS, :] = key[:, cols].astype(BF16)
        pay[(KV_HEADS + j) * ROWS : (KV_HEADS + j + 1) * ROWS, :] = value[:, cols].astype(BF16)
    doc = docs[...] + 1
    row = lax.broadcasted_iota(jnp.int32, (DOC_ROWS, ROWS), 0)
    digits = jnp.where(row == 0, doc // DIGIT, jnp.where(row == 1, doc % DIGIT, 0))
    pay[2 * KV_HEADS * ROWS :, :] = digits.astype(F32).astype(BF16)


def other_kv_kernel(other, own_pay, ks, vs, pay):
    x = other[...]
    parts = (dot(x, ks[...]).astype(BF16), dot(x, vs[...]).astype(BF16))
    for j in range(2 * KV_HEADS):
        pay[j * GROUP : j * GROUP + ROWS, :] = own_pay[j * ROWS : (j + 1) * ROWS, :]
        at = (j % KV_HEADS) * HEAD_SIZE
        pay[j * GROUP + ROWS : (j + 1) * GROUP, :] = parts[j // KV_HEADS][:, at : at + HEAD_SIZE]
    pay[2 * KV_HEADS * GROUP :, :] = own_pay[2 * KV_HEADS * ROWS :, :]


def query_kernel(own, other, w_query, pay, q_out, send):
    step = 2 * HEAD_SIZE
    send[Q_ROWS:, :] = pay[...]
    for i in range(HEADS // 2):
        w = w_query[:, i * step : (i + 1) * step]
        mine = dot(own[...], w).astype(BF16)
        theirs = dot(other[...], w).astype(BF16)
        for j in range(2):
            rows = pl.ds((2 * i + j) * ROWS, ROWS)
            cols = slice(j * HEAD_SIZE, (j + 1) * HEAD_SIZE)
            q_out[rows, :] = mine[:, cols]
            send[rows, :] = theirs[:, cols]


BASE = 2 * KV_HEADS * GROUP


def ids_of(ref, start=0):
    d = ref[start + BASE : start + BASE + DOC_ROWS, :].astype(F32)
    return d[0:1] * DIGIT + d[1:2]


def down(ids):
    return jnp.transpose(jnp.broadcast_to(ids, (ROWS, ROWS)))


def scores(q, k, bias):
    s = dot_t(q, k).reshape(SHARE, ROWS, k.shape[0]) * SCALE + bias[None]
    return s.reshape(SHARE * ROWS, k.shape[0])


def side_by_side(*blocks):
    return jnp.concatenate(blocks, axis=1)


def wide(x):
    return jnp.broadcast_to(x, (SHARE * ROWS, HEAD_SIZE))


def place(o, side, j, buf):
    for i in range(SHARE):
        col = (j * SHARE + i) * HEAD_SIZE
        buf[side, :, col : col + HEAD_SIZE] = o[i * ROWS : (i + 1) * ROWS, :]


def side_copy(buf, out, sem, side, j):
    width = SHARE * HEAD_SIZE
    start = jnp.where(lax.axis_index("head") == side, 0, HEADS * HEAD_SIZE) + j * width
    to = out.at[:, pl.ds(pl.multiple_of(start, width), width)]
    return pltpu.make_async_copy(buf.at[side, :, pl.ds(j * width, width)], to, sem.at[side, j])


def wait_all(buf, out, sem):
    for side in range(2):
        for j in range(KV_HEADS):
            side_copy(buf, out, sem, side, j).wait()


def near_kernel(late, q_mine, q_sent, pay, near_mine, near_sent, out, acc_out, m_out, l_out, flag, buf, sem):
    half = lax.axis_index("head")
    docs = ids_of(pay)
    doc_q = down(docs)
    r = lax.broadcasted_iota(jnp.int32, (ROWS, ROWS), 0)
    c = lax.broadcasted_iota(jnp.int32, (ROWS, ROWS), 1)
    here_a = jnp.where((doc_q == docs) & (c <= r), 0.0, NEG)
    here_b = jnp.where((doc_q == ids_of(q_sent, Q_ROWS)) & (c < half * ROWS), 0.0, NEG)
    near_a = jnp.where(doc_q == ids_of(near_mine), 0.0, NEG)
    near_b = jnp.where(doc_q == ids_of(near_sent), 0.0, NEG)

    def attend(final):
        for side in range(2):
            if side == 0:
                q_ref, here, start, near = q_mine, pay, 0, near_mine
                bias = side_by_side(here_a, here_b, near_a, near_b)
            else:
                q_ref, here, start, near = q_sent, q_sent, Q_ROWS, near_sent
                bias = side_by_side(here_b, here_a, near_b, near_a)

            def gather(j):
                at = j * GROUP
                return jnp.concatenate([here[pl.ds(start + at, GROUP), :], near[pl.ds(at, GROUP), :]], axis=0)

            for j in range(KV_HEADS):
                rows = pl.ds(j * SHARE * ROWS, SHARE * ROWS)
                s = scores(q_ref[rows, :], gather(j), bias)
                top = jnp.max(s, axis=1, keepdims=True)
                p = jnp.exp2(s - top)
                total = jnp.sum(p, axis=1, keepdims=True)
                acc = dot(p.astype(BF16), gather(KV_HEADS + j))
                if final:
                    place((acc / total).astype(BF16), side, j, buf)
                    side_copy(buf, out, sem, side, j).start()
                else:
                    to = pl.ds((side * HEADS + j * SHARE) * ROWS, SHARE * ROWS)
                    m_out[to, :] = wide(top)
                    l_out[to, :] = wide(total)
                    acc_out[to, :] = acc
        if final:
            wait_all(buf, out, sem)

    first = jnp.where(half == 0, ids_of(near_mine), ids_of(near_sent))
    more = jnp.min(first) == jnp.min(docs)
    flag[...] = jnp.where(more, 1.0, 0.0) * jnp.ones_like(flag)

    @pl.when(more)
    def _():
        attend(False)

    @pl.when(jnp.logical_not(more))
    def _():
        attend(True)


def far_kernel(q_mine, q_sent, pay, far_mine, far_sent, acc_in, m_in, l_in, flag, before, out, buf, sem):
    @pl.when(jnp.max(flag[...]) > 0.5)
    def _():
        doc_q = down(ids_of(pay))
        far_a = jnp.where(doc_q == ids_of(far_mine), 0.0, NEG)
        far_b = jnp.where(doc_q == ids_of(far_sent), 0.0, NEG)
        for side in range(2):
            q_ref = (q_mine, q_sent)[side]
            far = (far_mine, far_sent)[side]
            bias = side_by_side(far_a, far_b) if side == 0 else side_by_side(far_b, far_a)
            for j in range(KV_HEADS):
                rows = pl.ds(j * SHARE * ROWS, SHARE * ROWS)
                at = pl.ds((side * HEADS + j * SHARE) * ROWS, SHARE * ROWS)
                s = scores(q_ref[rows, :], far[pl.ds(j * GROUP, GROUP), :], bias)
                old = m_in[at, :]
                top = jnp.maximum(old, wide(jnp.max(s, axis=1, keepdims=True)))
                factor = jnp.exp2(old - top)
                p = jnp.exp2(s - jnp.concatenate([top, top], axis=1))
                total = l_in[at, :] * factor + wide(jnp.sum(p, axis=1, keepdims=True))
                acc = acc_in[at, :] * factor
                acc += dot(p.astype(BF16), far[pl.ds((KV_HEADS + j) * GROUP, GROUP), :])
                place((acc / total).astype(BF16), side, j, buf)
                side_copy(buf, out, sem, side, j).start()
        wait_all(buf, out, sem)


VMEM = pl.BlockSpec(memory_space=pltpu.VMEM)
ANY = pl.BlockSpec(memory_space=pl.ANY)
DMA = pltpu.SemaphoreType.DMA


def call(kernel, name, outs, ins, mib, flops, size, scratch=(), to=None, alias={}):
    many = isinstance(outs, list)
    return pl.pallas_call(
        kernel,
        out_shape=outs,
        in_specs=ins,
        out_specs=to or ([VMEM] * len(outs) if many else VMEM),
        input_output_aliases=alias,
        scratch_shapes=list(scratch),
        compiler_params=pltpu.CompilerParams(vmem_limit_bytes=mib << 20),
        cost_estimate=pl.CostEstimate(flops=flops, bytes_accessed=size, transcendentals=0),
        name=name,
    )


def bf16(*shape):
    return pltpu.VMEM(shape, BF16)


def fast(x):
    return pltpu.with_memory_space_constraint(x, pltpu.VMEM)


def on_device(tokens, doc_ids, w_query, w_key, value_weight):
    groups = lax.axis_size("srv")

    def swap(x):
        return lax.ppermute(x, "head", [(0, 1), (1, 0)])

    first = call(first_kernel, "first", bf16(DOC_ROWS, HEAD_SIZE), [], 1, 10**11, 10**11)()
    own, w_query, w_key, w_value = map(fast, (tokens, w_query, w_key, value_weight))
    other = swap(tokens)
    flops = 4 * ROWS * WIDTH * KV
    own_pay = call(
        own_kv_kernel,
        "own_kv",
        bf16(2 * KV_HEADS * ROWS + DOC_ROWS, HEAD_SIZE),
        [ANY] + [VMEM] * 4,
        16,
        flops,
        5 << 20,
    )(first, own, w_key, w_value, doc_ids.reshape(1, ROWS))
    pay = call(
        other_kv_kernel, "other_kv", bf16(PAY_ROWS, HEAD_SIZE), [VMEM] * 4, 16, flops, 5 << 20
    )(other, own_pay, w_key, w_value)
    near = lax.ppermute(pay, "srv", [(i, i + 1) for i in range(groups - 1)])
    far = lax.ppermute(pay, "srv", [(i, i + 2) for i in range(groups - 2)])
    q_mine, q_send = call(
        query_kernel,
        "query",
        [bf16(Q_ROWS, HEAD_SIZE), bf16(Q_ROWS + PAY_ROWS, HEAD_SIZE)],
        [VMEM] * 4,
        24,
        2 * GROUP * WIDTH * HEADS * HEAD_SIZE,
        11 << 20,
    )(own, other, w_query, pay)
    q_sent = swap(q_send)
    near_sent = swap(near)
    pairs = ROWS * GROUP * 2 * HEADS * HEAD_SIZE
    late = call(first_kernel, "late", bf16(DOC_ROWS, HEAD_SIZE), [ANY], 1, 10**11, 10**11)(pay)
    result = jax.ShapeDtypeStruct((ROWS, 2 * HEADS * HEAD_SIZE), BF16)
    sides = [pltpu.VMEM((2, ROWS, HEADS * HEAD_SIZE), BF16), DMA((2, KV_HEADS))]
    out, acc, m, l, flag = call(
        near_kernel,
        "attend_near",
        [result] + [pltpu.VMEM((2 * Q_ROWS, HEAD_SIZE), F32)] * 3 + [pltpu.VMEM((8, HEAD_SIZE), F32)],
        [ANY] + [VMEM] * 5,
        16,
        1,
        1,
        sides,
        [ANY] + [VMEM] * 4,
    )(late, q_mine, q_sent, pay, near, near_sent)
    far, l = lax.optimization_barrier((far, l))
    far_sent = swap(far)
    return call(
        far_kernel,
        "attend_far",
        result,
        [VMEM] * 9 + [ANY],
        16,
        4 * pairs,
        4 << 20,
        sides,
        ANY,
        {9: 0},
    )(q_mine, q_sent, pay, far, far_sent, acc, m, l, flag, out)


def solution(mesh):
    in_specs = (
        P(("srv", "head"), None),
        P(("srv", "head")),
        P(None, "head"),
        P(None, "head"),
        P(None, "head"),
    )
    out_specs = P(("srv", "head"), None)
    return jax.shard_map(
        on_device, mesh=mesh, in_specs=in_specs, out_specs=out_specs, check_vma=False
    )
```
